32 devices in a mesh: grp: 2 (over x), aux: 16 (over z, y, core).
Axes of the slice: x: 2, y: 2, z: 4, core: 2. Of those that a mesh axis runs over, the one named last changes fastest.
Arguments:
- gamma_half: bfloat16 [32, 16, 9216], P(('grp', 'aux')), parts along dimension 0, may hold values from -6 to 6
- c_occ: bfloat16 [18432, 1000], P(('grp', 'aux')), parts along dimension 0, may hold values from -1.5 to 1.5
- integrals: bfloat16 [32, 16, 128, 128], P(('grp', 'aux')), parts along dimension 0, may hold values from -0.125 to 0.125
- occ_batch: int32 [32], P('grp'), parts along dimension 0, may hold values from 0 to 999, as said below
- kept_blocks: int32 [32, 2], P('grp'), parts along dimension 0, may hold values from 0 to 71, as said below
- block_owner: int32 [32], P('grp'), parts along dimension 0, may hold values from 0 to 15, as said below
Outputs:
- gamma_blocks: bfloat16 [64, 16, 128, 128], P(('grp', 'aux')), parts along dimension 0
- lagrangian: float32 [32, 9216], P('grp', 'aux'), parts along dimension 0
The draws below stay inside these ranges and needn't reach their ends.
There are 2 independent parts, one for each index of `grp`. The reference program is written for one: setup_inputs(seed, part) draws one part's arguments, and reference() takes and returns one part's arrays. A program takes and returns all parts, laid end to end along the dimension named above; each array names one. Nothing has to cross between parts.
Inputs may be any that keep to these rules, and one draw needn't show every extreme that they name: `occ_batch`: distinct orbital indices. `kept_blocks`: distinct (row block, column block) pairs; the first min(16, 72) of them are diagonal pairs (r, r). `block_owner`: each owner is named by at most 2 blocks, and some owner by exactly 2.
All inputs are finite; a program needn't handle non-finite values.
Results may differ from the reference program's by a relative error of at most 0.001.
Values may be sent and summed in bfloat16 or wider, within the bound.
A program may use at most 64 MiB of HBM per device.

```python
import jax
import jax.numpy as jnp
from jax import lax

NBF = 9216
NOCC = 1000
OCC_B = 16
BS = 128
SLOTS = 2
NAUX = 16
OWNERS = 16
OWNER_SLOTS = 32
NKEPT = 16
NBLK = 72


def draw_occ_batch(key, part):
    key = jax.random.fold_in(key, 11)
    return jax.random.permutation(key, NOCC)[:OCC_B].astype(jnp.int32)


def draw_kept_blocks(key, part):
    key = jax.random.fold_in(key, 12)
    pair_total = NBLK * NBLK
    ranking = jax.random.permutation(key, pair_total).astype(jnp.int32)
    positions = jnp.arange(pair_total, dtype=jnp.int32)
    diagonal = positions // NBLK == positions % NBLK
    scores = jnp.where(diagonal, ranking - pair_total, ranking)
    picked = jnp.argsort(scores, stable=True)[:NKEPT].astype(jnp.int32)
    return jnp.stack([picked // NBLK, picked % NBLK], axis=1).astype(jnp.int32)


def draw_block_owner(key, part):
    key = jax.random.fold_in(key, 13)
    owner_key, slot_key = jax.random.split(key)
    pair_total = OWNERS * SLOTS
    ranking = jax.random.permutation(owner_key, pair_total).astype(jnp.int32)
    full_owner = jax.random.randint(slot_key, (), 0, OWNERS).astype(jnp.int32)
    positions = jnp.arange(pair_total, dtype=jnp.int32)
    scores = jnp.where(positions // SLOTS == full_owner, positions % SLOTS - SLOTS, ranking)
    picked = jnp.argsort(scores, stable=True)[:NKEPT].astype(jnp.int32)
    return (picked // SLOTS).astype(jnp.int32)


def steps_of(own_key, extent, cuts, least, high):
    def one(position, parts):
        draws = jax.random.uniform(jax.random.fold_in(jax.random.fold_in(own_key, 6), position), (parts,), jnp.float32, least / len(cuts), high / len(cuts))
        return jnp.repeat(jnp.exp(draws), extent[position] // parts).reshape((-1,) + (1,) * (len(extent) - position - 1))

    factor_of = one(*cuts[0])
    for cut in cuts[1:]:
        factor_of = factor_of * one(*cut)
    return factor_of


def noise(rng, shape, deviation, limit, shards=(), kind=jnp.bfloat16):
    array = jax.random.normal(rng, shape, jnp.float32) * deviation
    if len(shards) > 0:
        array = steps_of(rng, shape, shards, -0.22, 0.18) * array
    return jnp.clip(array, min=-limit, max=limit).astype(kind)


def setup_inputs(seed: int = 0, part: int = 0) -> dict:
    keys = jax.random.split(jax.random.key(seed), 7)
    part_splits = jax.random.split(jax.random.fold_in(keys[6], part), 7)
    return {
        "gamma_half": noise(part_splits[0], (NAUX, OCC_B, NBF), 1.0, 6.0, ((0, 16),)),
        "c_occ": noise(part_splits[1], (NBF, NOCC), 0.25, 1.5, ((0, 16),)),
        "integrals": noise(part_splits[2], (NAUX, NKEPT, BS, BS), (NAUX * BS * max(1, NKEPT // NBLK)) ** -0.5, 0.125, ((0, 16),)),
        "occ_batch": draw_occ_batch(jax.random.fold_in(jax.random.fold_in(keys[6], part), 71), part),
        "kept_blocks": draw_kept_blocks(jax.random.fold_in(jax.random.fold_in(keys[6], part), 71), part),
        "block_owner": draw_block_owner(jax.random.fold_in(jax.random.fold_in(keys[6], part), 71), part),
    }


def locate(block_owner, owner_count, slot_count):
    kept_count = block_owner.shape[0]
    indices = jnp.arange(kept_count, dtype=jnp.int32)
    earlier = (block_owner[:, None] == block_owner[None, :]) & (indices[None, :] < indices[:, None])
    slot_index = jnp.sum(earlier.astype(jnp.int32), axis=1).astype(jnp.int32)
    placed = block_owner * slot_count + slot_index
    target = jnp.arange(owner_count * slot_count, dtype=jnp.int32)
    matches = (placed[None, :] == target[:, None]).astype(jnp.int32)
    chosen = jnp.sum(matches * indices[None, :], axis=1).astype(jnp.int32)
    filled = jnp.sum(matches, axis=1).astype(jnp.int32)
    return chosen, filled


def reference(gamma_half, c_occ, integrals, occ_batch, kept_blocks, block_owner):
    occ_all = jnp.take(c_occ, occ_batch, axis=1)
    occ_tiles = occ_all.reshape(NBLK, BS, OCC_B)
    half_tiles = gamma_half.reshape(NAUX, OCC_B, NBLK, BS).transpose(2, 0, 1, 3)
    chosen, filled = locate(block_owner, OWNERS, SLOTS)

    def form_block(target_row):
        kept = chosen[target_row]
        left_tile = occ_tiles[kept_blocks[kept, 0]].astype(jnp.float32)
        right_tile = half_tiles[kept_blocks[kept, 1]].astype(jnp.float32)
        formed = jnp.einsum("xb,pby->pxy", left_tile, right_tile)
        formed = formed * filled[target_row].astype(jnp.float32)
        return formed.astype(jnp.bfloat16)

    gamma_blocks = lax.map(form_block, jnp.arange(OWNER_SLOTS, dtype=jnp.int32))

    def project_block(kept):
        slab = lax.dynamic_index_in_dim(integrals, kept, axis=1, keepdims=False).astype(jnp.float32)
        right_tile = half_tiles[kept_blocks[kept, 1]].astype(jnp.float32)
        return jnp.einsum("pxy,pby->bx", slab, right_tile)

    pieces = lax.map(project_block, jnp.arange(NKEPT, dtype=jnp.int32))
    onehot = (kept_blocks[None, :, 0] == jnp.arange(NBLK, dtype=jnp.int32)[:, None]).astype(jnp.float32)
    lagrangian = jnp.einsum("mk,kbx->bmx", onehot, pieces, precision=lax.Precision.HIGHEST).reshape(OCC_B, NBF)
    return (gamma_blocks, lagrangian)
```

```python
import functools

import jax
import jax.numpy as jnp
from jax import lax
from jax.experimental import pallas as pl
from jax.experimental.pallas import tpu as pltpu
from jax.sharding import PartitionSpec as P

SLOTS = 2
TILE = 8
UNROLL_LIMIT = 16
VMEM_BYTES = 32 * 1024 * 1024
MESH = pl.DeviceIdType.MESH


def loop(count, step, init):
    if count <= UNROLL_LIMIT:
        carry = init
        for index in range(count):
            carry = step(index, carry)
        return carry
    return lax.fori_loop(0, count, step, init)


def iota(shape, dimension):
    return lax.broadcasted_iota(jnp.int32, shape, dimension)


def exchange_kernel(
    dims,
    kept_ref,
    owner_ref,
    batch_ref,
    half_hbm,
    occ_hbm,
    integrals_hbm,
    tiles_out,
    result_out,
    half_v,
    occ_v,
    integrals_v,
    window_v,
    select_v,
    send_sums,
    recv_sums,
    send_tiles,
    send_result,
    load_sem,
    send_sem,
    recv_sem,
):
    devices, width, kept, rows, windows, edge, basis = dims
    groups = devices // width
    kept_part = kept // groups
    head = kept_part
    me = lax.axis_index("aux")
    grp = lax.axis_index("grp")
    my_group = me // width

    barrier = pltpu.get_barrier_semaphore()

    def greet(step, carry):
        peer = lax.rem(me + 1 + step, devices)
        pl.semaphore_signal(barrier, inc=1, device_id=(grp, peer), device_id_type=MESH)
        return carry

    load_half = pltpu.make_async_copy(half_hbm.at[0], half_v.at[:, pl.ds(0, basis)], load_sem.at[0])
    load_integrals = pltpu.make_async_copy(integrals_hbm.at[0], integrals_v, load_sem.at[1])
    load_occ = pltpu.make_async_copy(occ_hbm, occ_v, load_sem.at[2])
    load_half.start()
    load_integrals.start()
    load_occ.start()
    loop(devices - 1, greet, 0)

    half_v[:, pl.ds(basis, edge)] = jnp.zeros((width, edge), half_v.dtype)
    window_v[...] = jnp.zeros_like(window_v)

    split_lanes = 3 * kept_part
    lane_kept = lax.rem(iota((TILE, split_lanes), 1), kept_part)
    row_lane = jnp.full((TILE, split_lanes), -1, jnp.int32)
    for index in range(kept_part):
        row_lane = jnp.where(lane_kept == index, kept_ref[my_group * kept_part + index, 0], row_lane)
    lane_window = iota((TILE, devices * TILE), 1)
    window_index = lax.rem(lane_window, TILE)
    window_block = jnp.where(
        window_index < windows, ((lane_window // TILE) * rows) // edge + window_index, -5
    )
    sub_kept = iota((TILE, split_lanes), 0)
    sub_window = iota((TILE, devices * TILE), 0)

    load_half.wait()

    def place(dest, carry):
        def scan(step, found):
            index = kept - 1 - step
            col_a, row_a, col_b, row_b = found
            hit = owner_ref[index] == dest
            return (
                jnp.where(hit, kept_ref[index, 1], col_a),
                jnp.where(hit, kept_ref[index, 0], row_a),
                jnp.where(hit, col_a, col_b),
                jnp.where(hit, row_a, row_b),
            )

        col_a, row_a, col_b, row_b = loop(
            kept, scan, (jnp.int32(basis // edge), jnp.int32(-1), jnp.int32(basis // edge), jnp.int32(-1))
        )
        send_tiles[dest, pl.ds(0, width), :] = half_v[:, pl.ds(col_a * edge, edge)]
        send_tiles[dest, pl.ds(width, width), :] = half_v[:, pl.ds(col_b * edge, edge)]
        if groups > 1:
            mine = lax.rem(dest, groups) == my_group
            row_a = jnp.where(mine, row_a, -1)
            row_b = jnp.where(mine, row_b, -1)
        wanted = jnp.where(sub_window == windows, row_a, jnp.where(sub_window == windows + 1, row_b, -1))
        pick_occ = jnp.where(wanted == window_block, 1.0, 0.0)
        block = jnp.where(sub_kept < windows, (dest * rows) // edge + sub_kept, -5)
        pick_sum = jnp.where(block == row_lane, 1.0, 0.0)
        select_v[dest] = jnp.concatenate([pick_occ, pick_sum], axis=1)
        return carry

    loop(devices, place, 0)

    load_integrals.wait()
    for index in range(kept):
        group, place_in = index // kept_part, index % kept_part
        start = kept_ref[index, 1] * edge
        piece = lax.dot_general(
            half_v[:, pl.ds(start, edge)],
            integrals_v[index],
            (((1,), (1,)), ((), ())),
            preferred_element_type=jnp.float32,
        )
        send_sums[pl.ds(group * width, width), place_in, :] = piece

    load_occ.wait()
    orbitals = occ_v.shape[1]
    sub_batch = iota((width, 1), 0)
    batch = jnp.zeros((width, 1), jnp.int32)
    for index in range(width):
        batch = jnp.where(sub_batch == index, batch_ref[index], batch)
    pick = jnp.where(iota((width, orbitals), 1) == batch, 1.0, 0.0).astype(jnp.bfloat16)
    window_v[:, pl.ds(0, rows)] = lax.dot_general(
        pick, occ_v[...], (((1,), (1,)), ((), ())), preferred_element_type=jnp.float32
    )
    shifted = pltpu.roll(window_v[...], lax.rem(me * rows, edge), 1)
    for group in range(groups):
        for index in range(windows):
            send_sums[pl.ds(group * width, width), head + index, :] = shifted[
                :, index * edge : (index + 1) * edge
            ]
        for index in range(windows, TILE):
            send_sums[pl.ds(group * width, width), head + index, :] = jnp.zeros(
                (width, edge), jnp.float32
            )

    def sums_copy(peer):
        return pltpu.make_async_remote_copy(
            src_ref=send_sums.at[peer],
            dst_ref=recv_sums.at[me],
            send_sem=send_sem.at[0],
            recv_sem=recv_sem.at[0],
            device_id=(grp, peer),
            device_id_type=MESH,
        )

    def tiles_copy(peer):
        return pltpu.make_async_remote_copy(
            src_ref=send_tiles.at[peer],
            dst_ref=tiles_out.at[me],
            send_sem=send_sem.at[1],
            recv_sem=recv_sem.at[1],
            device_id=(grp, peer),
            device_id_type=MESH,
        )

    def result_copy(peer):
        return pltpu.make_async_remote_copy(
            src_ref=send_result.at[peer],
            dst_ref=result_out.at[me],
            send_sem=send_sem.at[2],
            recv_sem=recv_sem.at[2],
            device_id=(grp, peer),
            device_id_type=MESH,
        )

    def start_all(copy):
        def start(step, carry):
            copy(lax.rem(me + 1 + step, devices)).start()
            return carry

        loop(devices - 1, start, 0)

    def wait_all(buffer, sem):
        others = buffer.at[pl.ds(0, devices - 1)]
        pltpu.make_async_copy(others, others, sem).wait()

    pl.semaphore_wait(barrier, devices - 1)
    start_all(sums_copy)
    start_all(tiles_copy)
    recv_sums[me] = send_sums[me]
    tiles_out[me] = send_tiles[me]
    wait_all(recv_sums, recv_sem.at[0])

    total = jnp.sum(recv_sums[:, pl.ds(0, head), :], axis=0)
    high = total.astype(jnp.bfloat16)
    left = total - high.astype(jnp.float32)
    middle = left.astype(jnp.bfloat16)
    low = (left - middle.astype(jnp.float32)).astype(jnp.bfloat16)
    window_rows = recv_sums[:, pl.ds(head, TILE), :].reshape(devices * TILE, edge).astype(jnp.bfloat16)
    operand = jnp.concatenate([window_rows, high, middle, low], axis=0)
    select = select_v[...].reshape(devices * TILE, devices * TILE + split_lanes).astype(jnp.bfloat16)
    moved = jnp.dot(select, operand, preferred_element_type=jnp.float32)
    send_result[...] = moved.reshape(devices, TILE, edge)
    start_all(result_copy)
    result_out[me] = send_result[me]
    wait_all(tiles_out, recv_sem.at[1])
    wait_all(result_out, recv_sem.at[2])
    wait_all(send_sums, send_sem.at[0])
    wait_all(send_tiles, send_sem.at[1])
    wait_all(send_result, send_sem.at[2])


def finish_kernel(dims, tiles_ref, result_ref, blocks_hbm, lagrangian_ref, blocks_v, store_sem):
    devices, width, kept, rows, windows, edge, basis = dims
    me = lax.axis_index("aux")

    def row(index):
        return jnp.sum(result_ref[:, index, :].reshape(devices // width, width, edge), axis=0)

    for slot in range(SLOTS):
        left = row(windows + slot).T.astype(jnp.bfloat16)

        def form(index, carry):
            blocks_v[slot, index] = jnp.dot(
                left,
                tiles_ref[index, pl.ds(slot * width, width), :],
                preferred_element_type=jnp.float32,
            ).astype(jnp.bfloat16)
            return carry

        loop(devices, form, 0)
        pltpu.make_async_copy(blocks_v.at[slot], blocks_hbm.at[slot], store_sem.at[slot]).start()
    whole = jnp.concatenate([row(index) for index in range(windows)], axis=1)
    offset = lax.rem(me * rows, edge)
    whole = pltpu.roll(whole, lax.rem(windows * edge - offset, windows * edge), 1)
    lagrangian_ref[...] = whole[:, :rows]
    for slot in range(SLOTS):
        pltpu.make_async_copy(blocks_v.at[slot], blocks_hbm.at[slot], store_sem.at[slot]).wait()


def body(gamma_half, c_occ, integrals, occ_batch, kept_blocks, block_owner):
    devices = lax.axis_size("aux")
    aux_dev, width, basis = gamma_half.shape
    kept, edge = integrals.shape[1], integrals.shape[-1]
    rows, orbitals = c_occ.shape
    windows = max((index * rows % edge + rows + edge - 1) // edge for index in range(devices))
    assert aux_dev == 1 and devices % width == 0 and kept % (devices // width) == 0
    assert windows + SLOTS <= TILE
    dims = (devices, width, kept, rows, windows, edge, basis)
    kept_part = kept * width // devices
    sums = (devices, kept_part + TILE, edge)
    tiles = (devices, SLOTS * width, edge)
    result = (devices, TILE, edge)
    smem = pl.BlockSpec(memory_space=pltpu.SMEM)
    vmem = pl.BlockSpec(memory_space=pltpu.VMEM)
    anywhere = pl.BlockSpec(memory_space=pl.ANY)
    received, moved = pl.pallas_call(
        functools.partial(exchange_kernel, dims),
        out_shape=(
            jax.ShapeDtypeStruct(tiles, jnp.bfloat16),
            jax.ShapeDtypeStruct(result, jnp.float32),
        ),
        in_specs=[smem, smem, smem, anywhere, anywhere, anywhere],
        out_specs=(vmem, vmem),
        scratch_shapes=[
            pltpu.VMEM((width, basis + edge), jnp.bfloat16),
            pltpu.VMEM((rows, orbitals), jnp.bfloat16),
            pltpu.VMEM((kept, edge, edge), jnp.bfloat16),
            pltpu.VMEM((width, windows * edge), jnp.float32),
            pltpu.VMEM((devices, TILE, devices * TILE + 3 * kept_part), jnp.float32),
            pltpu.VMEM(sums, jnp.float32),
            pltpu.VMEM(sums, jnp.float32),
            pltpu.VMEM(tiles, jnp.bfloat16),
            pltpu.VMEM(result, jnp.float32),
            pltpu.SemaphoreType.DMA((3,)),
            pltpu.SemaphoreType.DMA((3,)),
            pltpu.SemaphoreType.DMA((3,)),
        ],
        compiler_params=pltpu.CompilerParams(
            collective_id=0, has_side_effects=True, vmem_limit_bytes=VMEM_BYTES
        ),
        name="exchange",
    )(kept_blocks, block_owner, occ_batch, gamma_half, c_occ, integrals)
    return pl.pallas_call(
        functools.partial(finish_kernel, dims),
        out_shape=(
            jax.ShapeDtypeStruct((SLOTS, devices, edge, edge), jnp.bfloat16),
            jax.ShapeDtypeStruct((width, rows), jnp.float32),
        ),
        in_specs=[vmem, vmem],
        out_specs=(anywhere, vmem),
        scratch_shapes=[
            pltpu.VMEM((SLOTS, devices, edge, edge), jnp.bfloat16),
            pltpu.SemaphoreType.DMA((SLOTS,)),
        ],
        compiler_params=pltpu.CompilerParams(vmem_limit_bytes=VMEM_BYTES),
        name="finish",
    )(received, moved)


def solution(mesh):
    return jax.shard_map(
        body,
        mesh=mesh,
        in_specs=(
            P(("grp", "aux"), None, None),
            P(("grp", "aux"), None),
            P(("grp", "aux"), None, None, None),
            P("grp"),
            P("grp", None),
            P("grp"),
        ),
        out_specs=(P(("grp", "aux"), None, None, None), P("grp", "aux")),
        check_vma=False,
    )
```

```python
import functools

import jax
import jax.numpy as jnp
from jax import lax
from jax.experimental import pallas as pl
from jax.experimental.pallas import tpu as pltpu
from jax.sharding import PartitionSpec as P

SLOTS = 2
TILE = 8
UNROLL_LIMIT = 16
VMEM_BYTES = 60 * 1024 * 1024
MESH = pl.DeviceIdType.MESH


def loop(count, step, init):
    if count <= UNROLL_LIMIT:
        carry = init
        for index in range(count):
            carry = step(index, carry)
        return carry
    return lax.fori_loop(0, count, step, init)


def iota(shape, dimension):
    return lax.broadcasted_iota(jnp.int32, shape, dimension)


def exchange_kernel(
    dims,
    kept_hbm,
    owner_hbm,
    batch_hbm,
    half_hbm,
    occ_hbm,
    integrals_hbm,
    tiles_out,
    result_out,
    kept_ref,
    owner_ref,
    batch_ref,
    half_v,
    occ_v,
    integrals_v,
    window_v,
    select_v,
    send_sums,
    recv_sums,
    send_tiles,
    send_result,
    load_sem,
    send_sem,
    recv_sem,
):
    devices, width, kept, rows, windows, edge, basis = dims
    groups = devices // width
    kept_part = kept // groups
    head = kept_part
    me = lax.axis_index("aux")
    grp = lax.axis_index("grp")
    my_group = me // width

    barrier = pltpu.get_barrier_semaphore()

    def greet(step, carry):
        peer = lax.rem(me + 1 + step, devices)
        pl.semaphore_signal(barrier, inc=1, device_id=(grp, peer), device_id_type=MESH)
        return carry

    load_kept = pltpu.make_async_copy(kept_hbm, kept_ref, load_sem.at[3])
    load_owner = pltpu.make_async_copy(owner_hbm, owner_ref, load_sem.at[4])
    load_batch = pltpu.make_async_copy(batch_hbm, batch_ref, load_sem.at[5])
    load_kept.start()
    load_owner.start()
    load_batch.start()
    load_half = pltpu.make_async_copy(half_hbm.at[0], half_v.at[:, pl.ds(0, basis)], load_sem.at[0])
    load_integrals = pltpu.make_async_copy(integrals_hbm.at[0], integrals_v, load_sem.at[1])
    load_occ = pltpu.make_async_copy(occ_hbm, occ_v, load_sem.at[2])
    load_half.start()
    load_integrals.start()
    load_occ.start()
    loop(devices - 1, greet, 0)

    half_v[:, pl.ds(basis, edge)] = jnp.zeros((width, edge), half_v.dtype)
    window_v[...] = jnp.zeros_like(window_v)

    load_kept.wait()
    load_owner.wait()
    load_batch.wait()

    split_lanes = 3 * kept_part
    lane_kept = lax.rem(iota((TILE, split_lanes), 1), kept_part)
    row_lane = jnp.full((TILE, split_lanes), -1, jnp.int32)
    for index in range(kept_part):
        row_lane = jnp.where(lane_kept == index, kept_ref[0, my_group * kept_part + index], row_lane)
    lane_window = iota((TILE, devices * TILE), 1)
    window_index = lax.rem(lane_window, TILE)
    window_block = jnp.where(
        window_index < windows, ((lane_window // TILE) * rows) // edge + window_index, -5
    )
    sub_kept = iota((TILE, split_lanes), 0)
    sub_window = iota((TILE, devices * TILE), 0)

    load_half.wait()

    def place(dest, carry):
        def scan(step, found):
            index = kept - 1 - step
            col_a, row_a, col_b, row_b = found
            hit = owner_ref[index] == dest
            return (
                jnp.where(hit, kept_ref[1, index], col_a),
                jnp.where(hit, kept_ref[0, index], row_a),
                jnp.where(hit, col_a, col_b),
                jnp.where(hit, row_a, row_b),
            )

        col_a, row_a, col_b, row_b = loop(
            kept, scan, (jnp.int32(basis // edge), jnp.int32(-1), jnp.int32(basis // edge), jnp.int32(-1))
        )
        send_tiles[dest, pl.ds(0, width), :] = half_v[:, pl.ds(col_a * edge, edge)]
        send_tiles[dest, pl.ds(width, width), :] = half_v[:, pl.ds(col_b * edge, edge)]
        if groups > 1:
            mine = lax.rem(dest, groups) == my_group
            row_a = jnp.where(mine, row_a, -1)
            row_b = jnp.where(mine, row_b, -1)
        wanted = jnp.where(sub_window == windows, row_a, jnp.where(sub_window == windows + 1, row_b, -1))
        pick_occ = jnp.where(wanted == window_block, 1.0, 0.0)
        block = jnp.where(sub_kept < windows, (dest * rows) // edge + sub_kept, -5)
        pick_sum = jnp.where(block == row_lane, 1.0, 0.0)
        select_v[dest] = jnp.concatenate([pick_occ, pick_sum], axis=1)
        return carry

    loop(devices, place, 0)

    load_integrals.wait()
    for index in range(kept):
        group, place_in = index // kept_part, index % kept_part
        start = kept_ref[1, index] * edge
        piece = lax.dot_general(
            half_v[:, pl.ds(start, edge)],
            integrals_v[index],
            (((1,), (1,)), ((), ())),
            preferred_element_type=jnp.float32,
        )
        send_sums[pl.ds(group * width, width), place_in, :] = piece

    load_occ.wait()
    orbitals = occ_v.shape[1]
    sub_batch = iota((width, 1), 0)
    batch = jnp.zeros((width, 1), jnp.int32)
    for index in range(width):
        batch = jnp.where(sub_batch == index, batch_ref[index], batch)
    pick = jnp.where(iota((width, orbitals), 1) == batch, 1.0, 0.0).astype(jnp.bfloat16)
    window_v[:, pl.ds(0, rows)] = lax.dot_general(
        pick, occ_v[...], (((1,), (1,)), ((), ())), preferred_element_type=jnp.float32
    )
    shifted = pltpu.roll(window_v[...], lax.rem(me * rows, edge), 1)
    for group in range(groups):
        for index in range(windows):
            send_sums[pl.ds(group * width, width), head + index, :] = shifted[
                :, index * edge : (index + 1) * edge
            ]
        for index in range(windows, TILE):
            send_sums[pl.ds(group * width, width), head + index, :] = jnp.zeros(
                (width, edge), jnp.float32
            )

    def sums_copy(peer):
        return pltpu.make_async_remote_copy(
            src_ref=send_sums.at[peer],
            dst_ref=recv_sums.at[me],
            send_sem=send_sem.at[0],
            recv_sem=recv_sem.at[0],
            device_id=(grp, peer),
            device_id_type=MESH,
        )

    def tiles_copy(peer):
        return pltpu.make_async_remote_copy(
            src_ref=send_tiles.at[peer],
            dst_ref=tiles_out.at[me],
            send_sem=send_sem.at[1],
            recv_sem=recv_sem.at[1],
            device_id=(grp, peer),
            device_id_type=MESH,
        )

    def result_copy(peer):
        return pltpu.make_async_remote_copy(
            src_ref=send_result.at[peer],
            dst_ref=result_out.at[me],
            send_sem=send_sem.at[2],
            recv_sem=recv_sem.at[2],
            device_id=(grp, peer),
            device_id_type=MESH,
        )

    def start_all(copy):
        def start(step, carry):
            copy(lax.rem(me + 1 + step, devices)).start()
            return carry

        loop(devices - 1, start, 0)

    def wait_all(buffer, sem):
        others = buffer.at[pl.ds(0, devices - 1)]
        pltpu.make_async_copy(others, others, sem).wait()

    pl.semaphore_wait(barrier, devices - 1)
    start_all(sums_copy)
    start_all(tiles_copy)
    recv_sums[me] = send_sums[me]
    tiles_out[me] = send_tiles[me]
    wait_all(recv_sums, recv_sem.at[0])

    total = jnp.sum(recv_sums[:, pl.ds(0, head), :], axis=0)
    high = total.astype(jnp.bfloat16)
    left = total - high.astype(jnp.float32)
    middle = left.astype(jnp.bfloat16)
    low = (left - middle.astype(jnp.float32)).astype(jnp.bfloat16)
    window_rows = recv_sums[:, pl.ds(head, TILE), :].reshape(devices * TILE, edge).astype(jnp.bfloat16)
    operand = jnp.concatenate([window_rows, high, middle, low], axis=0)
    select = select_v[...].reshape(devices * TILE, devices * TILE + split_lanes).astype(jnp.bfloat16)
    moved = jnp.dot(select, operand, preferred_element_type=jnp.float32)
    send_result[...] = moved.reshape(devices, TILE, edge)
    start_all(result_copy)
    result_out[me] = send_result[me]
    wait_all(tiles_out, recv_sem.at[1])
    wait_all(result_out, recv_sem.at[2])
    wait_all(send_sums, send_sem.at[0])
    wait_all(send_tiles, send_sem.at[1])
    wait_all(send_result, send_sem.at[2])


def finish_kernel(dims, tiles_ref, result_ref, blocks_hbm, lagrangian_ref, blocks_v, store_sem):
    devices, width, kept, rows, windows, edge, basis = dims
    me = lax.axis_index("aux")

    def row(index):
        return jnp.sum(result_ref[:, index, :].reshape(devices // width, width, edge), axis=0)

    for slot in range(SLOTS):
        left = row(windows + slot).T.astype(jnp.bfloat16)

        def form(index, carry):
            blocks_v[slot, index] = jnp.dot(
                left,
                tiles_ref[index, pl.ds(slot * width, width), :],
                preferred_element_type=jnp.float32,
            ).astype(jnp.bfloat16)
            return carry

        loop(devices, form, 0)
        pltpu.make_async_copy(blocks_v.at[slot], blocks_hbm.at[slot], store_sem.at[slot]).start()
    whole = jnp.concatenate([row(index) for index in range(windows)], axis=1)
    offset = lax.rem(me * rows, edge)
    whole = pltpu.roll(whole, lax.rem(windows * edge - offset, windows * edge), 1)
    lagrangian_ref[...] = whole[:, :rows]
    for slot in range(SLOTS):
        pltpu.make_async_copy(blocks_v.at[slot], blocks_hbm.at[slot], store_sem.at[slot]).wait()


def body(gamma_half, c_occ, integrals, occ_batch, kept_blocks, block_owner):
    devices = lax.axis_size("aux")
    aux_dev, width, basis = gamma_half.shape
    kept, edge = integrals.shape[1], integrals.shape[-1]
    rows, orbitals = c_occ.shape
    windows = max((index * rows % edge + rows + edge - 1) // edge for index in range(devices))
    assert aux_dev == 1 and devices % width == 0 and kept % (devices // width) == 0
    assert windows + SLOTS <= TILE
    dims = (devices, width, kept, rows, windows, edge, basis)
    kept_part = kept * width // devices
    sums = (devices, kept_part + TILE, edge)
    tiles = (devices, SLOTS * width, edge)
    result = (devices, TILE, edge)
    hbm = pl.BlockSpec(memory_space=pltpu.HBM)
    vmem = pl.BlockSpec(memory_space=pltpu.VMEM)
    anywhere = pl.BlockSpec(memory_space=pl.ANY)
    received, moved = pl.pallas_call(
        functools.partial(exchange_kernel, dims),
        out_shape=(
            jax.ShapeDtypeStruct(tiles, jnp.bfloat16),
            jax.ShapeDtypeStruct(result, jnp.float32),
        ),
        in_specs=[hbm] * 6,
        out_specs=(vmem, vmem),
        scratch_shapes=[
            pltpu.SMEM((2, kept), jnp.int32),
            pltpu.SMEM((kept,), jnp.int32),
            pltpu.SMEM((width,), jnp.int32),
            pltpu.VMEM((width, basis + edge), jnp.bfloat16),
            pltpu.VMEM((rows, orbitals), jnp.bfloat16),
            pltpu.VMEM((kept, edge, edge), jnp.bfloat16),
            pltpu.VMEM((width, windows * edge), jnp.float32),
            pltpu.VMEM((devices, TILE, devices * TILE + 3 * kept_part), jnp.float32),
            pltpu.VMEM(sums, jnp.float32),
            pltpu.VMEM(sums, jnp.float32),
            pltpu.VMEM(tiles, jnp.bfloat16),
            pltpu.VMEM(result, jnp.float32),
            pltpu.SemaphoreType.DMA((6,)),
            pltpu.SemaphoreType.DMA((3,)),
            pltpu.SemaphoreType.DMA((3,)),
        ],
        compiler_params=pltpu.CompilerParams(
            collective_id=0, has_side_effects=True, vmem_limit_bytes=VMEM_BYTES
        ),
        name="exchange",
    )(kept_blocks.T, block_owner, occ_batch, gamma_half, c_occ, integrals)
    return pl.pallas_call(
        functools.partial(finish_kernel, dims),
        out_shape=(
            jax.ShapeDtypeStruct((SLOTS, devices, edge, edge), jnp.bfloat16),
            jax.ShapeDtypeStruct((width, rows), jnp.float32),
        ),
        in_specs=[vmem, vmem],
        out_specs=(anywhere, vmem),
        scratch_shapes=[
            pltpu.VMEM((SLOTS, devices, edge, edge), jnp.bfloat16),
            pltpu.SemaphoreType.DMA((SLOTS,)),
        ],
        compiler_params=pltpu.CompilerParams(vmem_limit_bytes=VMEM_BYTES),
        name="finish",
    )(received, moved)


def solution(mesh):
    return jax.shard_map(
        body,
        mesh=mesh,
        in_specs=(
            P(("grp", "aux"), None, None),
            P(("grp", "aux"), None),
            P(("grp", "aux"), None, None, None),
            P("grp"),
            P("grp", None),
            P("grp"),
        ),
        out_specs=(P(("grp", "aux"), None, None, None), P("grp", "aux")),
        check_vma=False,
    )
```

```python
import functools

import jax
import jax.numpy as jnp
from jax import lax
from jax.experimental import pallas as pl
from jax.experimental.pallas import tpu as pltpu
from jax.sharding import PartitionSpec as P

SLOTS = 2
TILE = 8
UNROLL_LIMIT = 16
VMEM_BYTES = 60 * 1024 * 1024
MESH = pl.DeviceIdType.MESH


def loop(count, step, init):
    if count <= UNROLL_LIMIT:
        carry = init
        for index in range(count):
            carry = step(index, carry)
        return carry
    return lax.fori_loop(0, count, step, init)


def iota(shape, dimension):
    return lax.broadcasted_iota(jnp.int32, shape, dimension)


def exchange_kernel(
    dims,
    kept_hbm,
    owner_hbm,
    batch_hbm,
    half_hbm,
    occ_hbm,
    integrals_hbm,
    tiles_out,
    result_out,
    kept_ref,
    owner_ref,
    batch_ref,
    half_v,
    occ_v,
    integrals_v,
    window_v,
    select_v,
    send_sums,
    recv_sums,
    send_tiles,
    send_result,
    load_sem,
    send_sem,
    recv_sem,
):
    devices, width, kept, rows, windows, edge, basis = dims
    groups = devices // width
    kept_part = kept // groups
    head = kept_part
    me = lax.axis_index("aux")
    grp = lax.axis_index("grp")
    my_group = me // width

    barrier = pltpu.get_barrier_semaphore()

    def greet(step, carry):
        peer = lax.rem(me + 1 + step, devices)
        pl.semaphore_signal(barrier, inc=1, device_id=(grp, peer), device_id_type=MESH)
        return carry

    load_kept = pltpu.make_async_copy(kept_hbm, kept_ref, load_sem.at[3])
    load_owner = pltpu.make_async_copy(owner_hbm, owner_ref, load_sem.at[4])
    load_batch = pltpu.make_async_copy(batch_hbm, batch_ref, load_sem.at[5])
    load_kept.start()
    load_owner.start()
    load_batch.start()
    load_half = pltpu.make_async_copy(half_hbm.at[0], half_v.at[:, pl.ds(0, basis)], load_sem.at[0])
    load_integrals = pltpu.make_async_copy(integrals_hbm.at[0], integrals_v, load_sem.at[1])
    load_occ = pltpu.make_async_copy(occ_hbm, occ_v, load_sem.at[2])
    load_half.start()
    load_integrals.start()
    load_occ.start()
    loop(devices - 1, greet, 0)

    half_v[:, pl.ds(basis, edge)] = jnp.zeros((width, edge), half_v.dtype)
    window_v[...] = jnp.zeros_like(window_v)

    load_kept.wait()
    load_owner.wait()
    load_batch.wait()

    split_lanes = 3 * kept_part
    lane_kept = lax.rem(iota((TILE, split_lanes), 1), kept_part)
    row_lane = jnp.full((TILE, split_lanes), -1, jnp.int32)
    for index in range(kept_part):
        row_lane = jnp.where(lane_kept == index, kept_ref[0, my_group * kept_part + index], row_lane)
    lane_window = iota((TILE, devices * TILE), 1)
    window_index = lax.rem(lane_window, TILE)
    window_block = jnp.where(
        window_index < windows, ((lane_window // TILE) * rows) // edge + window_index, -5
    )
    sub_kept = iota((TILE, split_lanes), 0)
    sub_window = iota((TILE, devices * TILE), 0)

    load_half.wait()

    def owned(dest):
        def scan(step, found):
            index = kept - 1 - step
            col_a, row_a, col_b, row_b = found
            hit = owner_ref[index] == dest
            return (
                jnp.where(hit, kept_ref[1, index], col_a),
                jnp.where(hit, kept_ref[0, index], row_a),
                jnp.where(hit, col_a, col_b),
                jnp.where(hit, row_a, row_b),
            )

        return loop(
            kept,
            scan,
            (jnp.int32(basis // edge), jnp.int32(-1), jnp.int32(basis // edge), jnp.int32(-1)),
        )

    def fill_tiles(dest, carry):
        col_a, _, col_b, _ = owned(dest)
        send_tiles[dest, pl.ds(0, width), :] = half_v[:, pl.ds(col_a * edge, edge)]
        send_tiles[dest, pl.ds(width, width), :] = half_v[:, pl.ds(col_b * edge, edge)]
        return carry

    def fill_select(dest, carry):
        _, row_a, _, row_b = owned(dest)
        if groups > 1:
            mine = lax.rem(dest, groups) == my_group
            row_a = jnp.where(mine, row_a, -1)
            row_b = jnp.where(mine, row_b, -1)
        wanted = jnp.where(sub_window == windows, row_a, jnp.where(sub_window == windows + 1, row_b, -1))
        pick_occ = jnp.where(wanted == window_block, 1.0, 0.0)
        block = jnp.where(sub_kept < windows, (dest * rows) // edge + sub_kept, -5)
        pick_sum = jnp.where(block == row_lane, 1.0, 0.0)
        select_v[dest] = jnp.concatenate([pick_occ, pick_sum], axis=1)
        return carry

    load_integrals.wait()
    for index in range(kept):
        group, place_in = index // kept_part, index % kept_part
        start = kept_ref[1, index] * edge
        piece = lax.dot_general(
            half_v[:, pl.ds(start, edge)],
            integrals_v[index],
            (((1,), (1,)), ((), ())),
            preferred_element_type=jnp.float32,
        )
        send_sums[pl.ds(group * width, width), place_in, :] = piece

    load_occ.wait()
    orbitals = occ_v.shape[1]
    sub_batch = iota((width, 1), 0)
    batch = jnp.zeros((width, 1), jnp.int32)
    for index in range(width):
        batch = jnp.where(sub_batch == index, batch_ref[index], batch)
    pick = jnp.where(iota((width, orbitals), 1) == batch, 1.0, 0.0).astype(jnp.bfloat16)
    window_v[:, pl.ds(0, rows)] = lax.dot_general(
        pick, occ_v[...], (((1,), (1,)), ((), ())), preferred_element_type=jnp.float32
    )
    shifted = pltpu.roll(window_v[...], lax.rem(me * rows, edge), 1)
    for group in range(groups):
        for index in range(windows):
            send_sums[pl.ds(group * width, width), head + index, :] = shifted[
                :, index * edge : (index + 1) * edge
            ]
        for index in range(windows, TILE):
            send_sums[pl.ds(group * width, width), head + index, :] = jnp.zeros(
                (width, edge), jnp.float32
            )

    def sums_copy(peer):
        return pltpu.make_async_remote_copy(
            src_ref=send_sums.at[peer],
            dst_ref=recv_sums.at[me],
            send_sem=send_sem.at[0],
            recv_sem=recv_sem.at[0],
            device_id=(grp, peer),
            device_id_type=MESH,
        )

    def tiles_copy(peer):
        return pltpu.make_async_remote_copy(
            src_ref=send_tiles.at[peer],
            dst_ref=tiles_out.at[me],
            send_sem=send_sem.at[1],
            recv_sem=recv_sem.at[1],
            device_id=(grp, peer),
            device_id_type=MESH,
        )

    def result_copy(peer):
        return pltpu.make_async_remote_copy(
            src_ref=send_result.at[peer],
            dst_ref=result_out.at[me],
            send_sem=send_sem.at[2],
            recv_sem=recv_sem.at[2],
            device_id=(grp, peer),
            device_id_type=MESH,
        )

    def start_all(copy):
        def start(step, carry):
            copy(lax.rem(me + 1 + step, devices)).start()
            return carry

        loop(devices - 1, start, 0)

    def wait_all(buffer, sem):
        others = buffer.at[pl.ds(0, devices - 1)]
        pltpu.make_async_copy(others, others, sem).wait()

    pl.semaphore_wait(barrier, devices - 1)
    start_all(sums_copy)
    loop(devices, fill_tiles, 0)
    start_all(tiles_copy)
    loop(devices, fill_select, 0)
    recv_sums[me] = send_sums[me]
    tiles_out[me] = send_tiles[me]
    wait_all(recv_sums, recv_sem.at[0])

    total = jnp.sum(recv_sums[:, pl.ds(0, head), :], axis=0)
    high = total.astype(jnp.bfloat16)
    left = total - high.astype(jnp.float32)
    middle = left.astype(jnp.bfloat16)
    low = (left - middle.astype(jnp.float32)).astype(jnp.bfloat16)
    window_rows = recv_sums[:, pl.ds(head, TILE), :].reshape(devices * TILE, edge).astype(jnp.bfloat16)
    operand = jnp.concatenate([window_rows, high, middle, low], axis=0)
    select = select_v[...].reshape(devices * TILE, devices * TILE + split_lanes).astype(jnp.bfloat16)
    moved = jnp.dot(select, operand, preferred_element_type=jnp.float32)
    send_result[...] = moved.reshape(devices, TILE, edge)
    start_all(result_copy)
    result_out[me] = send_result[me]
    wait_all(tiles_out, recv_sem.at[1])
    wait_all(result_out, recv_sem.at[2])
    wait_all(send_sums, send_sem.at[0])
    wait_all(send_tiles, send_sem.at[1])
    wait_all(send_result, send_sem.at[2])


def finish_kernel(dims, tiles_ref, result_ref, blocks_hbm, lagrangian_ref, blocks_v, store_sem):
    devices, width, kept, rows, windows, edge, basis = dims
    me = lax.axis_index("aux")

    def row(index):
        return jnp.sum(result_ref[:, index, :].reshape(devices // width, width, edge), axis=0)

    for slot in range(SLOTS):
        left = row(windows + slot).T.astype(jnp.bfloat16)

        def form(index, carry):
            blocks_v[slot, index] = jnp.dot(
                left,
                tiles_ref[index, pl.ds(slot * width, width), :],
                preferred_element_type=jnp.float32,
            ).astype(jnp.bfloat16)
            return carry

        loop(devices, form, 0)
        pltpu.make_async_copy(blocks_v.at[slot], blocks_hbm.at[slot], store_sem.at[slot]).start()
    whole = jnp.concatenate([row(index) for index in range(windows)], axis=1)
    offset = lax.rem(me * rows, edge)
    whole = pltpu.roll(whole, lax.rem(windows * edge - offset, windows * edge), 1)
    lagrangian_ref[...] = whole[:, :rows]
    for slot in range(SLOTS):
        pltpu.make_async_copy(blocks_v.at[slot], blocks_hbm.at[slot], store_sem.at[slot]).wait()


def body(gamma_half, c_occ, integrals, occ_batch, kept_blocks, block_owner):
    devices = lax.axis_size("aux")
    aux_dev, width, basis = gamma_half.shape
    kept, edge = integrals.shape[1], integrals.shape[-1]
    rows, orbitals = c_occ.shape
    windows = max((index * rows % edge + rows + edge - 1) // edge for index in range(devices))
    assert aux_dev == 1 and devices % width == 0 and kept % (devices // width) == 0
    assert windows + SLOTS <= TILE
    dims = (devices, width, kept, rows, windows, edge, basis)
    kept_part = kept * width // devices
    sums = (devices, kept_part + TILE, edge)
    tiles = (devices, SLOTS * width, edge)
    result = (devices, TILE, edge)
    hbm = pl.BlockSpec(memory_space=pltpu.HBM)
    vmem = pl.BlockSpec(memory_space=pltpu.VMEM)
    anywhere = pl.BlockSpec(memory_space=pl.ANY)
    received, moved = pl.pallas_call(
        functools.partial(exchange_kernel, dims),
        out_shape=(
            pltpu.VMEM(tiles, jnp.bfloat16),
            pltpu.VMEM(result, jnp.float32),
        ),
        in_specs=[hbm] * 6,
        out_specs=(vmem, vmem),
        scratch_shapes=[
            pltpu.SMEM((2, kept), jnp.int32),
            pltpu.SMEM((kept,), jnp.int32),
            pltpu.SMEM((width,), jnp.int32),
            pltpu.VMEM((width, basis + edge), jnp.bfloat16),
            pltpu.VMEM((rows, orbitals), jnp.bfloat16),
            pltpu.VMEM((kept, edge, edge), jnp.bfloat16),
            pltpu.VMEM((width, windows * edge), jnp.float32),
            pltpu.VMEM((devices, TILE, devices * TILE + 3 * kept_part), jnp.float32),
            pltpu.VMEM(sums, jnp.float32),
            pltpu.VMEM(sums, jnp.float32),
            pltpu.VMEM(tiles, jnp.bfloat16),
            pltpu.VMEM(result, jnp.float32),
            pltpu.SemaphoreType.DMA((6,)),
            pltpu.SemaphoreType.DMA((3,)),
            pltpu.SemaphoreType.DMA((3,)),
        ],
        compiler_params=pltpu.CompilerParams(
            collective_id=0, has_side_effects=True, vmem_limit_bytes=VMEM_BYTES
        ),
        name="exchange",
    )(kept_blocks.T, block_owner, occ_batch, gamma_half, c_occ, integrals)
    return pl.pallas_call(
        functools.partial(finish_kernel, dims),
        out_shape=(
            jax.ShapeDtypeStruct((SLOTS, devices, edge, edge), jnp.bfloat16),
            jax.ShapeDtypeStruct((width, rows), jnp.float32),
        ),
        in_specs=[vmem, vmem],
        out_specs=(anywhere, vmem),
        scratch_shapes=[
            pltpu.VMEM((SLOTS, devices, edge, edge), jnp.bfloat16),
            pltpu.SemaphoreType.DMA((SLOTS,)),
        ],
        compiler_params=pltpu.CompilerParams(vmem_limit_bytes=VMEM_BYTES // 2),
        name="finish",
    )(received, moved)


def solution(mesh):
    return jax.shard_map(
        body,
        mesh=mesh,
        in_specs=(
            P(("grp", "aux"), None, None),
            P(("grp", "aux"), None),
            P(("grp", "aux"), None, None, None),
            P("grp"),
            P("grp", None),
            P("grp"),
        ),
        out_specs=(P(("grp", "aux"), None, None, None), P("grp", "aux")),
        check_vma=False,
    )
```

```python
import functools

import jax
import jax.numpy as jnp
from jax import lax
from jax.experimental import pallas as pl
from jax.experimental.pallas import tpu as pltpu
from jax.sharding import PartitionSpec as P

SLOTS = 2
TILE = 8
PARTS = 2
UNROLL_LIMIT = 16
VMEM_BYTES = 60 * 1024 * 1024
MESH = pl.DeviceIdType.MESH


def loop(count, step, init):
    if count <= UNROLL_LIMIT:
        carry = init
        for index in range(count):
            carry = step(index, carry)
        return carry
    return lax.fori_loop(0, count, step, init)


def iota(shape, dimension):
    return lax.broadcasted_iota(jnp.int32, shape, dimension)


def exchange_kernel(
    dims,
    kept_hbm,
    owner_hbm,
    batch_hbm,
    half_hbm,
    occ_hbm,
    integrals_hbm,
    tiles_out,
    result_out,
    kept_ref,
    owner_ref,
    batch_ref,
    half_v,
    occ_v,
    integrals_v,
    window_v,
    select_v,
    send_sums,
    recv_sums,
    send_tiles,
    send_result,
    load_sem,
    send_sem,
    recv_sem,
):
    devices, width, kept, rows, windows, edge, basis = dims
    groups = devices // width
    kept_part = kept // groups
    head = kept_part
    me = lax.axis_index("aux")
    grp = lax.axis_index("grp")
    my_group = me // width

    barrier = pltpu.get_barrier_semaphore()

    def greet(step, carry):
        peer = lax.rem(me + 1 + step, devices)
        pl.semaphore_signal(barrier, inc=1, device_id=(grp, peer), device_id_type=MESH)
        return carry

    load_kept = pltpu.make_async_copy(kept_hbm, kept_ref, load_sem.at[3])
    load_owner = pltpu.make_async_copy(owner_hbm, owner_ref, load_sem.at[4])
    load_batch = pltpu.make_async_copy(batch_hbm, batch_ref, load_sem.at[5])
    load_kept.start()
    load_owner.start()
    load_batch.start()
    load_half = pltpu.make_async_copy(half_hbm.at[0], half_v.at[:, pl.ds(0, basis)], load_sem.at[0])
    load_integrals = pltpu.make_async_copy(integrals_hbm.at[0], integrals_v, load_sem.at[1])
    load_occ = pltpu.make_async_copy(occ_hbm, occ_v, load_sem.at[2])
    load_half.start()
    load_integrals.start()
    load_occ.start()
    loop(devices - 1, greet, 0)

    half_v[:, pl.ds(basis, edge)] = jnp.zeros((width, edge), half_v.dtype)
    window_v[...] = jnp.zeros_like(window_v)

    load_kept.wait()
    load_owner.wait()
    load_batch.wait()

    split_lanes = 3 * kept_part
    lane_kept = lax.rem(iota((TILE, split_lanes), 1), kept_part)
    row_lane = jnp.full((TILE, split_lanes), -1, jnp.int32)
    for index in range(kept_part):
        row_lane = jnp.where(lane_kept == index, kept_ref[0, my_group * kept_part + index], row_lane)
    lane_window = iota((TILE, devices * TILE), 1)
    window_index = lax.rem(lane_window, TILE)
    window_block = jnp.where(
        window_index < windows, ((lane_window // TILE) * rows) // edge + window_index, -5
    )
    sub_kept = iota((TILE, split_lanes), 0)
    sub_window = iota((TILE, devices * TILE), 0)

    load_half.wait()

    def owned(dest):
        def scan(step, found):
            index = kept - 1 - step
            col_a, row_a, col_b, row_b = found
            hit = owner_ref[index] == dest
            return (
                jnp.where(hit, kept_ref[1, index], col_a),
                jnp.where(hit, kept_ref[0, index], row_a),
                jnp.where(hit, col_a, col_b),
                jnp.where(hit, row_a, row_b),
            )

        return loop(
            kept,
            scan,
            (jnp.int32(basis // edge), jnp.int32(-1), jnp.int32(basis // edge), jnp.int32(-1)),
        )

    def fill_tiles(dest, carry):
        col_a, _, col_b, _ = owned(dest)
        send_tiles[dest, pl.ds(0, width), :] = half_v[:, pl.ds(col_a * edge, edge)]
        send_tiles[dest, pl.ds(width, width), :] = half_v[:, pl.ds(col_b * edge, edge)]
        return carry

    def fill_select(dest, carry):
        _, row_a, _, row_b = owned(dest)
        if groups > 1:
            mine = lax.rem(dest, groups) == my_group
            row_a = jnp.where(mine, row_a, -1)
            row_b = jnp.where(mine, row_b, -1)
        wanted = jnp.where(sub_window == windows, row_a, jnp.where(sub_window == windows + 1, row_b, -1))
        pick_occ = jnp.where(wanted == window_block, 1.0, 0.0)
        block = jnp.where(sub_kept < windows, (dest * rows) // edge + sub_kept, -5)
        pick_sum = jnp.where(block == row_lane, 1.0, 0.0)
        select_v[dest] = jnp.concatenate([pick_occ, pick_sum], axis=1)
        return carry

    load_integrals.wait()
    for index in range(kept):
        group, place_in = index // kept_part, index % kept_part
        start = kept_ref[1, index] * edge
        piece = lax.dot_general(
            half_v[:, pl.ds(start, edge)],
            integrals_v[index],
            (((1,), (1,)), ((), ())),
            preferred_element_type=jnp.float32,
        )
        send_sums[pl.ds(group * width, width), place_in, :] = piece

    load_occ.wait()
    orbitals = occ_v.shape[1]
    sub_batch = iota((width, 1), 0)
    batch = jnp.zeros((width, 1), jnp.int32)
    for index in range(width):
        batch = jnp.where(sub_batch == index, batch_ref[index], batch)
    pick = jnp.where(iota((width, orbitals), 1) == batch, 1.0, 0.0).astype(jnp.bfloat16)
    window_v[:, pl.ds(0, rows)] = lax.dot_general(
        pick, occ_v[...], (((1,), (1,)), ((), ())), preferred_element_type=jnp.float32
    )
    shifted = pltpu.roll(window_v[...], lax.rem(me * rows, edge), 1)
    for group in range(groups):
        for index in range(windows):
            send_sums[pl.ds(group * width, width), head + index, :] = shifted[
                :, index * edge : (index + 1) * edge
            ]
        for index in range(windows, TILE):
            send_sums[pl.ds(group * width, width), head + index, :] = jnp.zeros(
                (width, edge), jnp.float32
            )

    def sums_copy(peer):
        return pltpu.make_async_remote_copy(
            src_ref=send_sums.at[peer],
            dst_ref=recv_sums.at[me],
            send_sem=send_sem.at[0],
            recv_sem=recv_sem.at[0],
            device_id=(grp, peer),
            device_id_type=MESH,
        )

    def tiles_copy(peer):
        return pltpu.make_async_remote_copy(
            src_ref=send_tiles.at[peer],
            dst_ref=tiles_out.at[me],
            send_sem=send_sem.at[1],
            recv_sem=recv_sem.at[1],
            device_id=(grp, peer),
            device_id_type=MESH,
        )

    def result_copy(peer):
        return pltpu.make_async_remote_copy(
            src_ref=send_result.at[peer],
            dst_ref=result_out.at[me],
            send_sem=send_sem.at[2],
            recv_sem=recv_sem.at[2],
            device_id=(grp, peer),
            device_id_type=MESH,
        )

    def start_all(copy):
        def start(step, carry):
            copy(lax.rem(me + 1 + step, devices)).start()
            return carry

        loop(devices - 1, start, 0)

    def wait_all(buffer, sem):
        others = buffer.at[pl.ds(0, devices - 1)]
        pltpu.make_async_copy(others, others, sem).wait()

    pl.semaphore_wait(barrier, devices - 1)
    start_all(sums_copy)
    loop(devices, fill_tiles, 0)
    start_all(tiles_copy)
    loop(devices, fill_select, 0)
    recv_sums[me] = send_sums[me]
    tiles_out[me] = send_tiles[me]
    wait_all(recv_sums, recv_sem.at[0])

    total = jnp.sum(recv_sums[:, pl.ds(0, head), :], axis=0)
    high = total.astype(jnp.bfloat16)
    left = total - high.astype(jnp.float32)
    middle = left.astype(jnp.bfloat16)
    low = (left - middle.astype(jnp.float32)).astype(jnp.bfloat16)
    window_rows = recv_sums[:, pl.ds(head, TILE), :].reshape(devices * TILE, edge).astype(jnp.bfloat16)
    operand = jnp.concatenate([window_rows, high, middle, low], axis=0)
    select = select_v[...].reshape(devices * TILE, devices * TILE + split_lanes).astype(jnp.bfloat16)
    moved = jnp.dot(select, operand, preferred_element_type=jnp.float32)
    send_result[...] = moved.reshape(devices, TILE, edge)
    start_all(result_copy)
    result_out[me] = send_result[me]
    wait_all(tiles_out, recv_sem.at[1])
    wait_all(result_out, recv_sem.at[2])
    wait_all(send_sums, send_sem.at[0])
    wait_all(send_tiles, send_sem.at[1])
    wait_all(send_result, send_sem.at[2])


def finish_kernel(dims, tiles_ref, result_ref, blocks_hbm, lagrangian_ref, blocks_v, store_sem):
    devices, width, kept, rows, windows, edge, basis = dims
    me = lax.axis_index("aux")

    def row(index):
        return jnp.sum(result_ref[:, index, :].reshape(devices // width, width, edge), axis=0)

    def store(slot, part):
        span = pl.ds(part * (devices // PARTS), devices // PARTS)
        return pltpu.make_async_copy(
            blocks_v.at[slot, span], blocks_hbm.at[slot, span], store_sem.at[slot * PARTS + part]
        )

    for slot in range(SLOTS):
        left = row(windows + slot).T.astype(jnp.bfloat16)

        def form(pair, carry):
            right = jnp.concatenate(
                [tiles_ref[2 * pair + half, pl.ds(slot * width, width), :] for half in range(2)], axis=1
            )
            both = jnp.dot(left, right, preferred_element_type=jnp.float32).astype(jnp.bfloat16)
            for half in range(2):
                blocks_v[slot, 2 * pair + half] = both[:, half * edge : (half + 1) * edge]
            return carry

        for part in range(PARTS):
            pairs = devices // 2 // PARTS
            loop(pairs, lambda step, carry: form(part * pairs + step, carry), 0)
            store(slot, part).start()
    whole = jnp.concatenate([row(index) for index in range(windows)], axis=1)
    offset = lax.rem(me * rows, edge)
    whole = pltpu.roll(whole, lax.rem(windows * edge - offset, windows * edge), 1)
    lagrangian_ref[...] = whole[:, :rows]
    for slot in range(SLOTS):
        for part in range(PARTS):
            store(slot, part).wait()


def body(gamma_half, c_occ, integrals, occ_batch, kept_blocks, block_owner):
    devices = lax.axis_size("aux")
    aux_dev, width, basis = gamma_half.shape
    kept, edge = integrals.shape[1], integrals.shape[-1]
    rows, orbitals = c_occ.shape
    windows = max((index * rows % edge + rows + edge - 1) // edge for index in range(devices))
    assert aux_dev == 1 and devices % width == 0 and kept % (devices // width) == 0
    assert windows + SLOTS <= TILE
    dims = (devices, width, kept, rows, windows, edge, basis)
    kept_part = kept * width // devices
    sums = (devices, kept_part + TILE, edge)
    tiles = (devices, SLOTS * width, edge)
    result = (devices, TILE, edge)
    hbm = pl.BlockSpec(memory_space=pltpu.HBM)
    vmem = pl.BlockSpec(memory_space=pltpu.VMEM)
    anywhere = pl.BlockSpec(memory_space=pl.ANY)
    received, moved = pl.pallas_call(
        functools.partial(exchange_kernel, dims),
        out_shape=(
            pltpu.VMEM(tiles, jnp.bfloat16),
            pltpu.VMEM(result, jnp.float32),
        ),
        in_specs=[hbm] * 6,
        out_specs=(vmem, vmem),
        scratch_shapes=[
            pltpu.SMEM((2, kept), jnp.int32),
            pltpu.SMEM((kept,), jnp.int32),
            pltpu.SMEM((width,), jnp.int32),
            pltpu.VMEM((width, basis + edge), jnp.bfloat16),
            pltpu.VMEM((rows, orbitals), jnp.bfloat16),
            pltpu.VMEM((kept, edge, edge), jnp.bfloat16),
            pltpu.VMEM((width, windows * edge), jnp.float32),
            pltpu.VMEM((devices, TILE, devices * TILE + 3 * kept_part), jnp.float32),
            pltpu.VMEM(sums, jnp.float32),
            pltpu.VMEM(sums, jnp.float32),
            pltpu.VMEM(tiles, jnp.bfloat16),
            pltpu.VMEM(result, jnp.float32),
            pltpu.SemaphoreType.DMA((6,)),
            pltpu.SemaphoreType.DMA((3,)),
            pltpu.SemaphoreType.DMA((3,)),
        ],
        compiler_params=pltpu.CompilerParams(
            collective_id=0, has_side_effects=True, vmem_limit_bytes=VMEM_BYTES
        ),
        name="exchange",
    )(kept_blocks.T, block_owner, occ_batch, gamma_half, c_occ, integrals)
    return pl.pallas_call(
        functools.partial(finish_kernel, dims),
        out_shape=(
            jax.ShapeDtypeStruct((SLOTS, devices, edge, edge), jnp.bfloat16),
            jax.ShapeDtypeStruct((width, rows), jnp.float32),
        ),
        in_specs=[vmem, vmem],
        out_specs=(anywhere, vmem),
        scratch_shapes=[
            pltpu.VMEM((SLOTS, devices, edge, edge), jnp.bfloat16),
            pltpu.SemaphoreType.DMA((SLOTS * PARTS,)),
        ],
        compiler_params=pltpu.CompilerParams(vmem_limit_bytes=VMEM_BYTES // 2),
        name="finish",
    )(received, moved)


def solution(mesh):
    return jax.shard_map(
        body,
        mesh=mesh,
        in_specs=(
            P(("grp", "aux"), None, None),
            P(("grp", "aux"), None),
            P(("grp", "aux"), None, None, None),
            P("grp"),
            P("grp", None),
            P("grp"),
        ),
        out_specs=(P(("grp", "aux"), None, None, None), P("grp", "aux")),
        check_vma=False,
    )
```
